32 devices in a mesh: section: 4 (over x, core), dp: 8 (over z, y).
Axes of the slice: x: 2, y: 2, z: 4, core: 2. Of those that a mesh axis runs over, the one named last changes fastest.
Arguments:
- value_weight: bfloat16 [4, 8192, 1024], P('section', 'dp'), may hold values from -0.0625 to 0.0625
- norm_gain: bfloat16 [4, 8192], P('section'), may hold values from 0.25 to 1.75
- mask_logits: bfloat16 [4, 6, 2048, 1024], P('section', None, 'dp'), may hold values from -5 to 5
- gumbel_noise: bfloat16 [4, 6, 2048, 1024], P('section', None, 'dp'), may hold values from -2.23 to 9.22, as said below
- stream_in: bfloat16 [2, 512, 8192], P(None, 'dp'), may hold values from -6 to 6
- stream_grad: bfloat16 [2, 512, 8192], P(None, 'dp'), may hold values from -6 to 6
Outputs:
- logit_grad: bfloat16 [4, 6, 2048, 1024], P('section', None, 'dp')
The draws below stay inside these ranges and needn't reach their ends.
Inputs may be any that keep to these rules, and one draw needn't show every extreme that they name: `gumbel_noise`: gumbel noise, minus the log of minus the log of a uniform number.
All inputs are finite; a program needn't handle non-finite values.
Results may differ from the reference program's by a relative error of at most 0.029.
Values may be sent and summed in bfloat16 or wider, within the bound.
A program may use at most 128 MiB of HBM per device.

```python
import jax
import jax.numpy as jnp
from jax import lax

D = 8192
KV = 1024
VHEADS = 8
MICRO = 2
TOK_DEV = 64
SECTIONS = 4
WORDPIECE_COUNT = 512


def draw_gumbel_noise(key, part):
    uniform = jax.random.uniform(key, (SECTIONS, 6, D // 4, KV), jnp.float32, 0.0001, 1.0 - 0.0001)
    return (-jnp.log(-jnp.log(uniform))).astype(jnp.bfloat16)


def level_of(stream_key, dims, shards, least, high):
    loudness, own = 1.0, jax.random.fold_in(stream_key, 6)
    for position, blocks in shards:
        heights = jnp.exp(jax.random.uniform(jax.random.fold_in(own, position), (blocks,), jnp.float32, least / len(shards), high / len(shards)))
        loudness = loudness * jnp.repeat(heights, dims[position] // blocks).reshape([-1 if axis == position else 1 for axis in range(len(dims))])
    return loudness


def bell_draw(own_key, dims, scale, reach, shards=(), dtype=jnp.bfloat16):
    entries = jax.random.normal(own_key, dims, jnp.float32) * scale
    if len(shards) > 0:
        entries = level_of(own_key, dims, shards, -0.22, 0.18) * entries
    return jnp.clip(entries, min=-reach, max=reach).astype(dtype)


def setup_inputs(seed: int = 0) -> dict:
    splits = jax.random.split(jax.random.key(seed), 7)
    return {
        "value_weight": bell_draw(splits[0], (SECTIONS, D, KV), D ** -0.5, 0.0625, ((0, 4), (1, 8))),
        "norm_gain": jnp.clip(1.0 + 0.15 * jax.random.normal(splits[1], (SECTIONS, D), jnp.float32), 0.25, 1.75).astype(jnp.bfloat16),
        "mask_logits": bell_draw(splits[2], (SECTIONS, 6, D // 4, KV), 1.5, 5.0, ((0, 4), (2, 8))),
        "gumbel_noise": draw_gumbel_noise(jax.random.fold_in(splits[6], 71), 0),
        "stream_in": bell_draw(splits[4], (MICRO, WORDPIECE_COUNT, D), 1.0, 6.0, ((1, 8),)),
        "stream_grad": bell_draw(splits[5], (MICRO, WORDPIECE_COUNT, D), 1.0, 6.0, ((1, 8),)),
    }


sharpness_divisor = 0.6666667
epsilon = 1e-05

def soft_mask(keeping_propensity, perturbed_draw):
    ranking_measure = (keeping_propensity.astype(jnp.float32) + perturbed_draw.astype(jnp.float32)) / sharpness_divisor
    expo = jnp.exp(ranking_measure)
    probs = expo / lax.optimization_barrier(jnp.sum(expo, axis=0))
    first = probs[0] + probs[1] + probs[2]
    second = probs[0] + probs[3] + probs[4]
    third = probs[1] + probs[3] + probs[5]
    fourth = probs[2] + probs[4] + probs[5]
    mask = jnp.stack([first, second, third, fourth], axis=1)
    return (probs, mask.reshape(-1, mask.shape[-1]))

def mask_logit_backward(probs, weight, grads):
    dmask = (grads * weight.astype(jnp.float32)).reshape(-1, 4, grads.shape[-1])
    row_a, row_b, row_c, row_d = (dmask[:, 0], dmask[:, 1], dmask[:, 2], dmask[:, 3])
    dprob = jnp.stack([row_a + row_b, row_a + row_c, row_a + row_d, row_b + row_c, row_b + row_d, row_c + row_d])
    ranking_derivative = probs * (dprob - lax.optimization_barrier(jnp.sum(probs * dprob, axis=0)))
    return (ranking_derivative / sharpness_divisor).astype(jnp.bfloat16)

def norm_forward(stream, gain):
    values = stream.astype(jnp.float32)
    scale = lax.rsqrt(lax.optimization_barrier(jnp.mean(values * values, axis=-1, keepdims=True)) + epsilon)
    normed = (values * scale * gain).astype(jnp.bfloat16)
    return (values, scale, normed)

def expand(value, width):
    count = value.shape[0]
    head = value.shape[1] // VHEADS
    repeat = width // value.shape[1]
    grown = jnp.broadcast_to(value.reshape(count, VHEADS, 1, head), (count, VHEADS, repeat, head))
    return grown.reshape(count, width)

def collapse(grad, kv_width):
    count, width = grad.shape
    head = kv_width // VHEADS
    repeat = width // kv_width
    return lax.optimization_barrier(jnp.sum(grad.reshape(count, VHEADS, repeat, head), axis=2)).reshape(count, kv_width)

def norm_backward(values, scale, gain, dnormed):
    scaled = dnormed * gain
    return scale * scaled - values * (scale * scale * scale) * lax.optimization_barrier(jnp.mean(scaled * values, axis=-1, keepdims=True))

def reference(value_weight, norm_gain, mask_logits, gumbel_noise, stream_in, stream_grad):
    sections = value_weight.shape[0]
    micro, wordpiece_total, width = stream_in.shape
    kv_width = value_weight.shape[2]
    devices = wordpiece_total // TOK_DEV
    probs_list = []
    weights = []
    for layer in range(sections):
        probs, mask = soft_mask(mask_logits[layer], gumbel_noise[layer])
        probs_list.append(probs)
        weights.append((value_weight[layer].astype(jnp.float32) * mask).astype(jnp.bfloat16))
    saved_x = [[None] * micro for layer in range(sections)]
    saved_u = [[None] * micro for layer in range(sections)]
    saved_g = [[None] * micro for layer in range(sections)]
    for batch in range(micro):
        stream = stream_in[batch]
        for layer in range(sections):
            gain = norm_gain[layer].astype(jnp.float32)
            values, scale, normed = norm_forward(stream, gain)
            saved_x[layer][batch] = stream
            saved_u[layer][batch] = normed
            value = jnp.dot(normed, weights[layer], preferred_element_type=jnp.float32)
            stream = (values + expand(value, width)).astype(jnp.bfloat16)
    for batch in range(micro):
        grad = stream_grad[batch]
        for layer in range(sections - 1, -1, -1):
            gain = norm_gain[layer].astype(jnp.float32)
            upper = grad.astype(jnp.float32)
            vgrad = collapse(upper, kv_width).astype(jnp.bfloat16)
            saved_g[layer][batch] = vgrad
            dnormed = lax.dot_general(vgrad, weights[layer], (((1,), (1,)), ((), ())), preferred_element_type=jnp.float32)
            values, scale, normed = norm_forward(saved_x[layer][batch], gain)
            grad = (upper + norm_backward(values, scale, gain, dnormed)).astype(jnp.bfloat16)
    results = []
    for layer in range(sections):
        inputs = jnp.stack(saved_u[layer]).reshape(micro, devices, TOK_DEV, width)
        inputs = jnp.transpose(inputs, (1, 0, 2, 3)).reshape(devices, micro * TOK_DEV, width)
        payload_derivatives = jnp.stack(saved_g[layer]).reshape(micro, devices, TOK_DEV, kv_width)
        payload_derivatives = jnp.transpose(payload_derivatives, (1, 0, 2, 3)).reshape(devices, micro * TOK_DEV, kv_width)

        def absorb(total, pair):
            term = lax.dot_general(pair[0], pair[1], (((0,), (0,)), ((), ())), preferred_element_type=jnp.float32)
            rounded = lax.optimization_barrier(term.astype(jnp.bfloat16))
            return (total + rounded.astype(jnp.float32), None)
        wgrad, discarded_value = lax.scan(absorb, jnp.zeros((width, kv_width), jnp.float32), (inputs, payload_derivatives))
        results.append(mask_logit_backward(probs_list[layer], value_weight[layer], wgrad))
    return jnp.stack(results)
```

```python
import jax
import jax.numpy as jnp
from jax import lax
from jax.sharding import PartitionSpec as P

VHEADS = 8


sharpness_divisor = 0.6666667
epsilon = 1e-05
F32 = jnp.float32
BF16 = jnp.bfloat16


def soft_mask(keeping_propensity, perturbed_draw):
    ranking_measure = (keeping_propensity.astype(F32) + perturbed_draw.astype(F32)) / sharpness_divisor
    expo = jnp.exp(ranking_measure)
    probs = expo / jnp.sum(expo, axis=0)
    first = probs[0] + probs[1] + probs[2]
    second = probs[0] + probs[3] + probs[4]
    third = probs[1] + probs[3] + probs[5]
    fourth = probs[2] + probs[4] + probs[5]
    mask = jnp.stack([first, second, third, fourth], axis=1)
    return (probs, mask.reshape(-1, mask.shape[-1]))


def mask_logit_backward(probs, weight, grads):
    dmask = (grads * weight.astype(F32)).reshape(-1, 4, grads.shape[-1])
    row_a, row_b, row_c, row_d = (dmask[:, 0], dmask[:, 1], dmask[:, 2], dmask[:, 3])
    dprob = jnp.stack([row_a + row_b, row_a + row_c, row_a + row_d, row_b + row_c, row_b + row_d, row_c + row_d])
    ranking_derivative = probs * (dprob - jnp.sum(probs * dprob, axis=0))
    return (ranking_derivative / sharpness_divisor).astype(BF16)


def collapse(x, kv_width):
    count, width = x.shape
    head = kv_width // VHEADS
    return jnp.sum(x.astype(F32).reshape(count, VHEADS, width // kv_width, head), axis=2).reshape(count, kv_width)


def dot(a, b, contract):
    return lax.dot_general(a, b, (contract, ((), ())), preferred_element_type=F32)


def per_device(value_weight, norm_gain, mask_logits, gumbel_noise, stream_in, stream_grad):
    section = lax.axis_index("section")
    sections = lax.axis_size("section")
    index, parts = lax.axis_index("dp"), lax.axis_size("dp")
    micro, rows, width = stream_in.shape
    weight = value_weight[0]
    block, kv = weight.shape
    head = kv // VHEADS
    repeat = width // kv
    local = min(block // head, repeat)
    heads = block // (local * head)
    sharers = parts * heads // VHEADS
    tokens = micro * rows
    x0 = stream_in.reshape(tokens, width)

    spread = lax.all_to_all(x0, "dp", split_axis=1, concat_axis=0, tiled=True)
    probs, mask = soft_mask(mask_logits[0], gumbel_noise[0])
    masked = (weight.astype(F32) * mask).astype(BF16)
    gain = lax.dynamic_slice_in_dim(norm_gain[0], index * block, block, 0).astype(F32)
    core = jnp.sum((masked.astype(F32) * gain[:, None]).reshape(heads, local, head, kv), axis=1).astype(BF16)
    cores = lax.all_gather(core.reshape(heads * head, kv), ("section", "dp"), axis=0, tiled=True)
    cores = cores.reshape(sections, VHEADS, sharers, head, kv)
    if sharers > 1:
        cores = jnp.sum(cores.astype(F32), axis=2).astype(BF16)
    cores = cores.reshape(sections, kv, kv)

    lhs = (spread.astype(F32) * gain).astype(BF16)
    part = dot(lhs, masked, ((1,), (0,))).astype(BF16)
    first = lax.psum_scatter(part, "dp", scatter_dimension=0, tiled=True)
    firsts = lax.all_gather(first, "section", axis=0, tiled=False).astype(F32)

    folded = collapse(x0, kv)
    square = jnp.sum(jnp.square(x0.astype(F32)), axis=1, keepdims=True)
    total = jnp.zeros((tokens, kv), F32)
    totals, scales, values = [], [], []
    for layer in range(sections):
        mean = square + 2 * jnp.sum(total * folded, axis=1, keepdims=True)
        mean = (mean + repeat * jnp.sum(total * total, axis=1, keepdims=True)) / width
        scale = lax.rsqrt(jnp.maximum(mean, 0) + epsilon)
        value = firsts[layer]
        if layer > 0:
            value = value + dot(total.astype(BF16), cores[layer], ((1,), (0,)))
        value = value * scale
        totals.append(total)
        scales.append(scale)
        values.append(value)
        total = total + value
    mine = lax.dynamic_index_in_dim(jnp.stack(totals), section, 0, keepdims=False).astype(BF16)
    mine = jnp.repeat(mine.reshape(tokens, parts // sharers, heads * head), sharers, axis=1)
    mine = mine.reshape(tokens, parts * heads * head)
    shift = lax.all_to_all(mine, "dp", split_axis=1, concat_axis=0, tiled=True)
    grad = collapse(stream_grad.reshape(tokens, width), kv)
    grads = [None] * sections
    for layer in range(sections - 1, -1, -1):
        vgrad = grad.astype(BF16)
        scale = scales[layer]
        grads[layer] = (vgrad.astype(F32) * scale).astype(BF16)
        if layer > 0:
            along = jnp.sum(vgrad.astype(F32) * values[layer], axis=1, keepdims=True) / width
            grad = grad + scale * dot(vgrad, cores[layer], ((1,), (1,)))
            grad = grad - scale * scale * along * (folded + repeat * totals[layer])
    sent = lax.dynamic_index_in_dim(jnp.stack(grads), section, 0, keepdims=False)
    right = lax.all_gather(sent, "dp", axis=0, tiled=True)

    count = right.shape[0]
    grown = jnp.broadcast_to(shift.reshape(count, heads, 1, head), (count, heads, local, head)).reshape(count, block)
    left = (spread.astype(F32) + grown.astype(F32)).astype(BF16)
    wgrad = dot(left, right, ((0,), (0,))) * gain[:, None]
    return mask_logit_backward(probs, weight, wgrad)[None]


def solution(mesh):
    return jax.shard_map(
        per_device,
        mesh=mesh,
        in_specs=(
            P("section", "dp", None),
            P("section", None),
            P("section", None, "dp", None),
            P("section", None, "dp", None),
            P(None, "dp", None),
            P(None, "dp", None),
        ),
        out_specs=P("section", None, "dp", None),
        check_vma=False,
    )
```

```python
import functools

import jax
import jax.numpy as jnp
from jax import lax
from jax.experimental import pallas as pl
from jax.experimental.pallas import tpu as pltpu
from jax.sharding import PartitionSpec as P

VHEADS = 8


sharpness_divisor = 0.6666667
epsilon = 1e-05
F32 = jnp.float32
BF16 = jnp.bfloat16
MESH = pl.DeviceIdType.MESH
LIMIT = 60 * 1024 * 1024


def dot(a, b, contract):
    return lax.dot_general(a, b, (contract, ((), ())), preferred_element_type=F32)


def planar(size):
    feature = lax.broadcasted_iota(jnp.int32, (size, size), 0)
    position = lax.broadcasted_iota(jnp.int32, (size, size), 1)
    groups = size // 4
    return (feature == 4 * (position % groups) + position // groups).astype(F32).astype(BF16)


def pattern_probs(logits_ref, noise_ref):
    scores = [
        jnp.exp((logits_ref[k].astype(F32) + noise_ref[k].astype(F32)) / sharpness_divisor) for k in range(6)
    ]
    inverse = 1.0 / (scores[0] + scores[1] + scores[2] + scores[3] + scores[4] + scores[5])
    return [score * inverse for score in scores]


def mask_kernel(local, head, logits_ref, noise_ref, weight_ref, gain_ref, masked_ref, core_ref, total):
    size = weight_ref.shape[0]
    groups = size // 4
    order = planar(size)
    p = pattern_probs(logits_ref, noise_ref)
    planes = [p[0] + p[1] + p[2], p[0] + p[3] + p[4], p[1] + p[3] + p[5], p[2] + p[4] + p[5]]
    apart = dot(order, weight_ref[...], ((0,), (0,)))
    rows = [(apart[r * groups:(r + 1) * groups] * planes[r]).astype(BF16) for r in range(4)]
    masked = dot(order, jnp.concatenate(rows, axis=0), ((1,), (0,)))
    masked_ref[...] = masked.astype(BF16)
    term = masked * gain_ref[...]

    @pl.when(pl.program_id(0) % local == 0)
    def _():
        total[...] = term

    @pl.when(pl.program_id(0) % local != 0)
    def _():
        total[...] += term

    core_ref[...] = total[...].astype(BF16)


def logit_kernel(logits_ref, noise_ref, weight_ref, gain_ref, spread_ref, shift_ref, right_ref, out_ref):
    size = weight_ref.shape[0]
    groups = size // 4
    order = planar(size)
    left = (spread_ref[...].astype(F32) + shift_ref[...].astype(F32)) * gain_ref[...]
    left = dot(left.astype(BF16), order, ((1,), (0,))).astype(BF16)
    wgrad = dot(left, right_ref[...], ((0,), (0,)))
    grad = wgrad * dot(order, weight_ref[...], ((0,), (0,)))
    a, b, c, d = [grad[r * groups:(r + 1) * groups] for r in range(4)]
    p = pattern_probs(logits_ref, noise_ref)
    dprob = [a + b, a + c, a + d, b + c, b + d, c + d]
    mean = sum(p[k] * dprob[k] for k in range(6))
    for k in range(6):
        out_ref[k] = (p[k] * (dprob[k] - mean) / sharpness_divisor).astype(BF16)


def relay_kernel(
    n, sections, sharers, x0_ref, top_ref, gain_ref, masked_ref, core_ref, spread_ref, shift_ref, right_ref,
    cores, parts, fromy, fromz, sums, full, hop, mine,
    a_send, a_recv, b_send, b_recv, c_send, c_recv, d_send, y_send, y_recv, z_send, z_recv,
    h_send, h_recv, v_send, v_recv, g_send, g_recv, f_send, own_sem,
):
    me, sec = lax.axis_index("dp"), lax.axis_index("section")
    half_n = n // 2
    lane = me % 2
    mate = me + 1 - 2 * lane
    twin = sec + 1 - 2 * (sec % 2)
    tokens, width = x0_ref.shape
    block = spread_ref.shape[2]
    kv = masked_ref.shape[1]
    head = kv // VHEADS
    repeat = width // kv
    half = tokens // 2

    def at(k):
        return lax.rem(me + k + n, n)

    barrier = pltpu.get_barrier_semaphore()

    @pl.loop(1, n)
    def _(k):
        pl.semaphore_signal(barrier, inc=1, device_id=(sec, at(k)), device_id_type=MESH)

    for step in (1, sections - 1):
        pl.semaphore_signal(barrier, inc=1, device_id=(lax.rem(sec + step, sections), me), device_id_type=MESH)
    pl.semaphore_wait(barrier, n + 1)

    def copy(src, dst, send, recv, where):
        return pltpu.make_async_remote_copy(
            src_ref=src, dst_ref=dst, send_sem=send, recv_sem=recv, device_id=where, device_id_type=MESH
        )

    rows = pl.ds(pl.multiple_of((sec % 2) * half, half), half)
    others = pl.ds(pl.multiple_of((1 - sec % 2) * half, half), half)

    def spread_out(k):
        dest = at(k)
        cols = pl.ds(pl.multiple_of(dest * block, block), block)
        return copy(x0_ref.at[rows, cols], spread_ref.at[me, rows], a_send.at[k], a_recv.at[me], (sec, dest))

    def spread_in(src):
        return copy(spread_ref.at[src, rows], spread_ref.at[src, rows], a_send.at[0], a_recv.at[src], (sec, mate))

    def twin_out(src):
        return copy(spread_ref.at[src, rows], spread_ref.at[src, rows], b_send.at[src], b_recv.at[src], (twin, me))

    def twin_in(src):
        return copy(spread_ref.at[src, others], spread_ref.at[src, others], b_send.at[src], b_recv.at[src], (twin, me))

    own_cols = pl.ds(pl.multiple_of(me * block, block), block)
    own = pltpu.make_async_copy(x0_ref.at[:, own_cols], spread_ref.at[me], own_sem)
    own.start()

    @pl.loop(1, n)
    def _(k):
        spread_out(k).start()

    def gather_out(buf, send, recv, k):
        return copy(buf.at[me], buf.at[me], send.at[k], recv.at[me], (sec, at(2 * k)))

    def gather_pass(buf, send, recv, k):
        src = at(-2 * k)
        return copy(buf.at[src], buf.at[src], send.at[k], recv.at[src], (sec, mate))

    def gather_in(buf, send, recv, src):
        return copy(buf.at[src], buf.at[src], send.at[0], recv.at[src], (sec, mate))

    def gather_start(buf, send, more, recv):
        gather_pass(buf, more, recv, 0).start()

        @pl.loop(1, half_n)
        def _(k):
            gather_out(buf, send, recv, k).start()

    def gather_forward(buf, send, more, recv, k):
        gather_in(buf, send, recv, at(-2 * k)).wait_recv()
        gather_pass(buf, more, recv, k).start()

    def gather_end(buf, send, more, recv):
        @pl.loop(0, half_n)
        def _(k):
            pair = at(-2 * k)
            gather_in(buf, send, recv, pair + 1 - 2 * lane).wait_recv()
            gather_pass(buf, more, recv, k).wait_send()

        @pl.loop(1, half_n)
        def _(k):
            gather_out(buf, send, recv, k).wait_send()

    cores[me] = core_ref[...]
    gather_start(cores, c_send, d_send, c_recv)

    def product(src):
        lhs = (spread_ref[src].astype(F32) * gain_ref[...]).astype(BF16)
        parts[src] = dot(lhs, masked_ref[...], ((1,), (0,))).astype(BF16)

    def mate_out(owner):
        return copy(parts.at[owner], fromy.at[owner // 2], y_send.at[owner // 2], y_recv.at[owner // 2], (sec, mate))

    def mate_in(owner):
        return copy(parts.at[owner], fromy.at[owner // 2], y_send.at[owner // 2], y_recv.at[owner // 2], (sec, mate))

    def arrive(k):
        src = at(-k)
        spread_in(src).wait_recv()
        twin_out(src).start()

    def whole(k):
        src = at(-k)
        twin_in(src).wait_recv()
        product(src)

    arrive(1)

    @pl.loop(1, half_n)
    def _(j):
        arrive(2 * j)
        whole(2 * j - 1)
        mate_out(at(1 - 2 * j)).start()
        arrive(2 * j + 1)
        whole(2 * j)
        gather_forward(cores, c_send, d_send, c_recv, j)

    whole(n - 1)
    mate_out(at(1 - n)).start()
    own.wait()
    product(me)

    folded = []
    tops = []
    square = jnp.zeros((tokens, 1), F32)
    for h in range(VHEADS):
        low = jnp.zeros((tokens, head), F32)
        high = jnp.zeros((tokens, head), F32)
        power = jnp.zeros((tokens, head), F32)
        for r in range(repeat):
            cols = slice((h * repeat + r) * head, (h * repeat + r + 1) * head)
            x = x0_ref[:, cols].astype(F32)
            low = low + x
            power = power + x * x
            high = high + top_ref[:, cols].astype(F32)
        folded.append(low)
        tops.append(high)
        square = square + jnp.sum(power, axis=1, keepdims=True)
    sums[...] = jnp.concatenate(folded, axis=1)
    hop[0] = jnp.concatenate(tops, axis=1).astype(BF16)

    def lane_out(k):
        owner = at(2 * k)
        return copy(parts.at[owner], fromz.at[me // 2], z_send.at[k], z_recv.at[me // 2], (sec, owner))

    def lane_in(src):
        return copy(parts.at[src], fromz.at[src // 2], z_send.at[0], z_recv.at[src // 2], (sec, mate))

    @pl.loop(1, half_n)
    def _(j):
        k = half_n - j
        owner = at(2 * k)
        mate_in(owner).wait_recv()
        parts[owner] = (parts[owner].astype(F32) + fromy[owner // 2].astype(F32)).astype(BF16)
        lane_out(k).start()

    mate_in(me).wait_recv()
    full[...] = parts[me].astype(F32) + fromy[me // 2].astype(F32)

    @pl.loop(1, half_n)
    def _(k):
        src = at(-2 * k)
        lane_in(src).wait_recv()
        full[...] += fromz[src // 2].astype(F32)

    gather_end(cores, c_send, d_send, c_recv)

    def core():
        if sharers == 1:
            return cores[...].reshape(kv, kv)
        group = cores[...].astype(F32).reshape(kv // cores.shape[1], sharers, cores.shape[1], kv)
        return jnp.sum(group, axis=1).astype(BF16).reshape(kv, kv)

    up = lax.rem(sec + 1, sections)
    down = lax.rem(sec + sections - 1, sections)

    @pl.when(sec == 0)
    def _():
        hop[2] = jnp.zeros((tokens, kv), BF16)

    @pl.when(sec > 0)
    def _():
        copy(mine, hop.at[2], h_send.at[0], h_recv.at[0], (down, me)).wait_recv()

    total = hop[2].astype(F32)
    mean = square + 2 * jnp.sum(total * sums[...], axis=1, keepdims=True)
    mean = (mean + repeat * jnp.sum(total * total, axis=1, keepdims=True)) / width
    scale = lax.rsqrt(jnp.maximum(mean, 0) + epsilon)
    full[...] = (full[...] + dot(hop[2], core(), ((1,), (0,)))) * scale
    mine[...] = (total + full[...]).astype(BF16)

    @pl.when(sec < sections - 1)
    def _():
        copy(mine, hop.at[2], h_send.at[0], h_recv.at[0], (up, me)).start()

    share = shift_ref.shape[2]

    def share_of(dest):
        return pl.ds(pl.multiple_of((dest // sharers) * share, share), share)

    def shift_out(k):
        dest = at(k)
        return copy(hop.at[2, :, share_of(dest)], shift_ref.at[me], v_send.at[k], v_recv.at[me], (sec, dest))

    @pl.loop(1, n)
    def _(k):
        shift_out(k).start()

    local = pltpu.make_async_copy(hop.at[2, :, share_of(me)], shift_ref.at[me], own_sem)
    local.start()

    @pl.when(sec == sections - 1)
    def _():
        hop[1] = hop[0]

    @pl.when(sec < sections - 1)
    def _():
        copy(hop.at[3], hop.at[1], h_send.at[1], h_recv.at[1], (up, me)).wait_recv()

    vgrad = hop[1].astype(F32)

    @pl.when(sec > 0)
    def _():
        along = jnp.sum(vgrad * full[...], axis=1, keepdims=True) / width
        below = vgrad + scale * dot(hop[1], core(), ((1,), (1,)))
        below = below - scale * scale * along * (sums[...] + repeat * hop[2].astype(F32))
        hop[3] = below.astype(BF16)
        copy(hop.at[3], hop.at[1], h_send.at[1], h_recv.at[1], (down, me)).start()

    right_ref[me] = (vgrad * scale).astype(BF16)
    gather_start(right_ref, g_send, f_send, g_recv)

    @pl.loop(1, half_n)
    def _(k):
        gather_forward(right_ref, g_send, f_send, g_recv, k)

    gather_end(right_ref, g_send, f_send, g_recv)
    local.wait()

    @pl.when(sec < sections - 1)
    def _():
        copy(mine, hop.at[2], h_send.at[0], h_recv.at[0], (up, me)).wait_send()

    @pl.when(sec > 0)
    def _():
        copy(hop.at[3], hop.at[1], h_send.at[1], h_recv.at[1], (down, me)).wait_send()

    @pl.loop(1, n)
    def _(k):
        src = at(-k)
        copy(hop.at[2, :, share_of(me)], shift_ref.at[src], v_send.at[k], v_recv.at[src], (sec, src)).wait_recv()
        shift_out(k).wait_send()
        spread_out(k).wait_send()
        twin_out(src).wait_send()

    @pl.loop(0, half_n)
    def _(k):
        mate_out(at(2 * k + 1)).wait_send()

    @pl.loop(1, half_n)
    def _(k):
        lane_out(k).wait_send()


def per_device(value_weight, norm_gain, mask_logits, gumbel_noise, stream_in, stream_grad):
    sections = lax.axis_size("section")
    index, n = lax.axis_index("dp"), lax.axis_size("dp")
    micro, rows, width = stream_in.shape
    weight, logits, noise = value_weight[0], mask_logits[0], gumbel_noise[0]
    block, kv = weight.shape
    head = kv // VHEADS
    repeat = width // kv
    local = min(block // head, repeat)
    heads = block // (local * head)
    sharers = n * heads // VHEADS
    share = heads * head
    tokens = micro * rows
    count = n * tokens
    gain = lax.dynamic_slice_in_dim(norm_gain[0], index * block, block, 0).astype(F32)
    steps = block // head
    pattern = pl.BlockSpec((6, head // 4, kv), lambda i: (0, i, 0))
    strip = pl.BlockSpec((head, kv), lambda i: (i, 0))

    masked, core = pl.pallas_call(
        functools.partial(mask_kernel, local, head),
        grid=(steps,),
        out_shape=[jax.ShapeDtypeStruct((block, kv), BF16), jax.ShapeDtypeStruct((share, kv), BF16)],
        in_specs=[pattern, pattern, strip, pl.BlockSpec((head, 1), lambda i: (i, 0))],
        out_specs=[strip, pl.BlockSpec((head, kv), lambda i: (i // local, 0))],
        scratch_shapes=[pltpu.VMEM((head, kv), F32)],
        compiler_params=pltpu.CompilerParams(vmem_limit_bytes=LIMIT),
        name="masks",
    )(logits, noise, weight, gain[:, None])

    dma = pltpu.SemaphoreType.DMA
    vmem = pl.BlockSpec(memory_space=pltpu.VMEM)
    spread, shift, right = pl.pallas_call(
        functools.partial(relay_kernel, n, sections, sharers),
        out_shape=[
            jax.ShapeDtypeStruct((n, tokens, block), BF16),
            jax.ShapeDtypeStruct((n, tokens, share), BF16),
            jax.ShapeDtypeStruct((n, tokens, kv), BF16),
        ],
        in_specs=[vmem] * 5,
        out_specs=[vmem] * 3,
        scratch_shapes=[
            pltpu.VMEM((n, share, kv), BF16),
            pltpu.VMEM((n, tokens, kv), BF16),
            pltpu.VMEM((n // 2, tokens, kv), BF16),
            pltpu.VMEM((n // 2, tokens, kv), BF16),
            pltpu.VMEM((tokens, kv), F32),
            pltpu.VMEM((tokens, kv), F32),
            pltpu.VMEM((4, tokens, kv), BF16),
            pltpu.VMEM((tokens, kv), BF16),
            dma((n,)), dma((n,)), dma((n,)), dma((n,)), dma((n,)), dma((n,)), dma((n,)),
            dma((n,)), dma((n,)), dma((n,)), dma((n,)), dma((2,)), dma((2,)),
            dma((n,)), dma((n,)), dma((n,)), dma((n,)), dma((n,)), dma,
        ],
        compiler_params=pltpu.CompilerParams(collective_id=0, has_side_effects=True, vmem_limit_bytes=LIMIT),
        name="relay",
    )(stream_in.reshape(tokens, width), stream_grad.reshape(tokens, width), gain[None], masked, core)

    out = pl.pallas_call(
        logit_kernel,
        grid=(steps,),
        out_shape=jax.ShapeDtypeStruct(logits.shape, BF16),
        in_specs=[
            pattern,
            pattern,
            strip,
            pl.BlockSpec((1, head), lambda i: (0, i)),
            pl.BlockSpec((count, head), lambda i: (0, i)),
            pl.BlockSpec((count, head), lambda i: (0, i // local)),
            pl.BlockSpec((count, kv), lambda i: (0, 0)),
        ],
        out_specs=pattern,
        compiler_params=pltpu.CompilerParams(vmem_limit_bytes=LIMIT),
        name="logits",
    )(logits, noise, weight, gain[None], spread.reshape(count, block), shift.reshape(count, share), right.reshape(count, kv))
    return out[None]


def solution(mesh):
    return jax.shard_map(
        per_device,
        mesh=mesh,
        in_specs=(
            P("section", "dp", None),
            P("section", None),
            P("section", None, "dp", None),
            P("section", None, "dp", None),
            P(None, "dp", None),
            P(None, "dp", None),
        ),
        out_specs=P("section", None, "dp", None),
        check_vma=False,
    )
```

```python
import functools

import jax
import jax.numpy as jnp
from jax import lax
from jax.experimental import pallas as pl
from jax.experimental.pallas import tpu as pltpu
from jax.sharding import PartitionSpec as P

VHEADS = 8


sharpness_divisor = 0.6666667
epsilon = 1e-05
F32 = jnp.float32
BF16 = jnp.bfloat16
MESH = pl.DeviceIdType.MESH
LIMIT = 60 * 1024 * 1024


def dot(a, b, contract):
    return lax.dot_general(a, b, (contract, ((), ())), preferred_element_type=F32)


def planar(size):
    feature = lax.broadcasted_iota(jnp.int32, (size, size), 0)
    position = lax.broadcasted_iota(jnp.int32, (size, size), 1)
    groups = size // 4
    return (feature == 4 * (position % groups) + position // groups).astype(F32).astype(BF16)


def pattern_probs(logits_ref, noise_ref):
    scores = [
        jnp.exp((logits_ref[k].astype(F32) + noise_ref[k].astype(F32)) / sharpness_divisor) for k in range(6)
    ]
    inverse = 1.0 / (scores[0] + scores[1] + scores[2] + scores[3] + scores[4] + scores[5])
    return [score * inverse for score in scores]


def mask_kernel(local, head, logits_ref, noise_ref, weight_ref, gain_ref, masked_ref, core_ref, total):
    size = weight_ref.shape[0]
    groups = size // 4
    order = planar(size)
    p = pattern_probs(logits_ref, noise_ref)
    planes = [p[0] + p[1] + p[2], p[0] + p[3] + p[4], p[1] + p[3] + p[5], p[2] + p[4] + p[5]]
    apart = dot(order, weight_ref[...], ((0,), (0,)))
    rows = [(apart[r * groups:(r + 1) * groups] * planes[r]).astype(BF16) for r in range(4)]
    masked = dot(order, jnp.concatenate(rows, axis=0), ((1,), (0,)))
    masked_ref[...] = masked.astype(BF16)
    term = masked * gain_ref[...]

    @pl.when(pl.program_id(0) % local == 0)
    def _():
        total[...] = term

    @pl.when(pl.program_id(0) % local != 0)
    def _():
        total[...] += term

    core_ref[...] = total[...].astype(BF16)


def logit_kernel(logits_ref, noise_ref, weight_ref, gain_ref, spread_ref, shift_ref, right_ref, out_ref):
    size = weight_ref.shape[0]
    groups = size // 4
    order = planar(size)
    left = (spread_ref[...].astype(F32) + shift_ref[...].astype(F32)) * gain_ref[...]
    left = dot(left.astype(BF16), order, ((1,), (0,))).astype(BF16)
    wgrad = dot(left, right_ref[...], ((0,), (0,)))
    grad = wgrad * dot(order, weight_ref[...], ((0,), (0,)))
    a, b, c, d = [grad[r * groups:(r + 1) * groups] for r in range(4)]
    p = pattern_probs(logits_ref, noise_ref)
    dprob = [a + b, a + c, a + d, b + c, b + d, c + d]
    mean = sum(p[k] * dprob[k] for k in range(6))
    for k in range(6):
        out_ref[k] = (p[k] * (dprob[k] - mean) / sharpness_divisor).astype(BF16)


def relay_kernel(
    n, sections, sharers, x0_ref, top_ref, gain_ref, masked_ref, core_ref, spread_ref, shift_ref, right_ref,
    cores, parts, fromy, fromz, sums, full, hop, mine,
    a_send, a_recv, b_send, b_recv, e_send, e_recv, p_send, p_recv, c_send, c_recv, d_send, y_send, y_recv, z_send, z_recv,
    h_send, h_recv, v_send, v_recv, g_send, g_recv, f_send, own_sem,
):
    me, sec = lax.axis_index("dp"), lax.axis_index("section")
    half_n = n // 2
    lane = me % 2
    mate = me + 1 - 2 * lane
    twin = sec + 1 - 2 * (sec % 2)
    tokens, width = x0_ref.shape
    block = spread_ref.shape[2]
    kv = masked_ref.shape[1]
    head = kv // VHEADS
    repeat = width // kv
    quarter = tokens // 4
    across = lax.rem(sec + 2, sections)
    beyond = lax.rem(twin + 2, sections)
    place = me // 2

    def at(k):
        return lax.rem(me + k + n, n)

    barrier = pltpu.get_barrier_semaphore()

    @pl.loop(1, n)
    def _(k):
        pl.semaphore_signal(barrier, inc=1, device_id=(sec, at(k)), device_id_type=MESH)

    for step in range(1, sections):
        pl.semaphore_signal(barrier, inc=1, device_id=(lax.rem(sec + step, sections), me), device_id_type=MESH)
    pl.semaphore_wait(barrier, n + sections - 2)

    def copy(src, dst, send, recv, where):
        return pltpu.make_async_remote_copy(
            src_ref=src, dst_ref=dst, send_sem=send, recv_sem=recv, device_id=where, device_id_type=MESH
        )

    def quarter_of(which):
        return pl.ds(pl.multiple_of(which * quarter, quarter), quarter)

    def spread_out(k):
        dest = at(k)
        cols = pl.ds(pl.multiple_of(dest * block, block), block)
        rows = quarter_of(sec)
        return copy(x0_ref.at[rows, cols], spread_ref.at[me, rows], a_send.at[k], a_recv.at[me], (sec, dest))

    def share(src, which, send, recv, to):
        ref = spread_ref.at[src, quarter_of(which)]
        return copy(ref, ref, send.at[src], recv.at[src], (to, me))

    def spread_in(src):
        ref = spread_ref.at[src, quarter_of(sec)]
        return copy(ref, ref, a_send.at[0], a_recv.at[src], (sec, mate))

    own_cols = pl.ds(pl.multiple_of(me * block, block), block)
    own = pltpu.make_async_copy(x0_ref.at[:, own_cols], spread_ref.at[me], own_sem)
    own.start()

    @pl.loop(1, n)
    def _(k):
        spread_out(k).start()

    def lane_copy(buf, send, recv, src, slot, dest):
        return copy(buf.at[src], buf.at[src], send.at[slot], recv.at[src], (sec, dest))

    def to_right(buf, send, recv, src, slot):
        return lane_copy(buf, send, recv, src, slot, lax.rem(me + 2, n))

    def to_left(buf, send, recv, src, slot):
        return lane_copy(buf, send, recv, src, slot, lax.rem(me + n - 2, n))

    def gather_pass(buf, more, recv, src):
        return lane_copy(buf, more, recv, src, src, mate)

    def gather_start(buf, send, more, recv):
        @pl.when(place < half_n - 1)
        def _():
            to_right(buf, send, recv, me, me).start()

        @pl.when(place > 0)
        def _():
            to_left(buf, send, recv, me, mate).start()

        gather_pass(buf, more, recv, me).start()

    def gather_forward(buf, send, more, recv, k):
        @pl.when(place >= k)
        def _():
            src = me - 2 * k
            gather_pass(buf, more, recv, src).wait_recv()

            @pl.when(place < half_n - 1)
            def _():
                to_right(buf, send, recv, src, src).start()

            gather_pass(buf, more, recv, src).start()

        @pl.when(place + k < half_n)
        def _():
            src = me + 2 * k
            gather_pass(buf, more, recv, src).wait_recv()

            @pl.when(place > 0)
            def _():
                to_left(buf, send, recv, src, src).start()

            gather_pass(buf, more, recv, src).start()

    def gather_end(buf, send, more, recv):
        @pl.loop(0, half_n)
        def _(k):
            src = 2 * k + lane
            gather_pass(buf, more, recv, 2 * k + 1 - lane).wait_recv()
            gather_pass(buf, more, recv, src).wait_send()

            @pl.when((k <= place) & (place < half_n - 1))
            def _():
                to_right(buf, send, recv, src, src).wait_send()

            @pl.when((k > place) & (place > 0))
            def _():
                to_left(buf, send, recv, src, src).wait_send()

        @pl.when(place > 0)
        def _():
            to_left(buf, send, recv, me, mate).wait_send()

    cores[me] = core_ref[...]
    gather_start(cores, c_send, d_send, c_recv)

    def product(src):
        lhs = (spread_ref[src].astype(F32) * gain_ref[...]).astype(BF16)
        parts[src] = dot(lhs, masked_ref[...], ((1,), (0,))).astype(BF16)

    def mate_out(owner):
        return copy(parts.at[owner], fromy.at[owner // 2], y_send.at[owner // 2], y_recv.at[owner // 2], (sec, mate))

    def mate_in(owner):
        return copy(parts.at[owner], fromy.at[owner // 2], y_send.at[owner // 2], y_recv.at[owner // 2], (sec, mate))

    def arrive(k):
        src = at(-k)
        spread_in(src).wait_recv()
        share(src, sec, e_send, e_recv, across).start()
        share(src, sec, b_send, b_recv, twin).start()

    def cross(k):
        src = at(-k)
        share(src, across, e_send, e_recv, across).wait_recv()
        share(src, across, p_send, p_recv, twin).start()

    def whole(k):
        src = at(-k)
        share(src, twin, b_send, b_recv, twin).wait_recv()
        share(src, beyond, p_send, p_recv, twin).wait_recv()
        product(src)

    arrive(1)
    arrive(2)
    cross(1)

    @pl.loop(1, half_n)
    def _(j):
        arrive(2 * j + 1)
        cross(2 * j)
        whole(2 * j - 1)
        mate_out(at(1 - 2 * j)).start()

        @pl.when(j < half_n - 1)
        def _():
            arrive(2 * j + 2)

        cross(2 * j + 1)
        whole(2 * j)
        gather_forward(cores, c_send, d_send, c_recv, j)

    whole(n - 1)
    mate_out(at(1 - n)).start()
    own.wait()
    product(me)

    folded = []
    tops = []
    square = jnp.zeros((tokens, 1), F32)
    for h in range(VHEADS):
        low = jnp.zeros((tokens, head), F32)
        high = jnp.zeros((tokens, head), F32)
        power = jnp.zeros((tokens, head), F32)
        for r in range(repeat):
            cols = slice((h * repeat + r) * head, (h * repeat + r + 1) * head)
            x = x0_ref[:, cols].astype(F32)
            low = low + x
            power = power + x * x
            high = high + top_ref[:, cols].astype(F32)
        folded.append(low)
        tops.append(high)
        square = square + jnp.sum(power, axis=1, keepdims=True)
    sums[...] = jnp.concatenate(folded, axis=1)
    hop[0] = jnp.concatenate(tops, axis=1).astype(BF16)

    def lane_out(k):
        owner = at(2 * k)
        return copy(parts.at[owner], fromz.at[me // 2], z_send.at[k], z_recv.at[me // 2], (sec, owner))

    def lane_in(src):
        return copy(parts.at[src], fromz.at[src // 2], z_send.at[0], z_recv.at[src // 2], (sec, mate))

    @pl.loop(1, half_n)
    def _(j):
        k = half_n - j
        owner = at(2 * k)
        mate_in(owner).wait_recv()
        parts[owner] = (parts[owner].astype(F32) + fromy[owner // 2].astype(F32)).astype(BF16)
        lane_out(k).start()

    mate_in(me).wait_recv()
    full[...] = parts[me].astype(F32) + fromy[me // 2].astype(F32)

    @pl.loop(1, half_n)
    def _(k):
        src = at(-2 * k)
        lane_in(src).wait_recv()
        full[...] += fromz[src // 2].astype(F32)

    gather_end(cores, c_send, d_send, c_recv)

    def core():
        if sharers == 1:
            return cores[...].reshape(kv, kv)
        group = cores[...].astype(F32).reshape(kv // cores.shape[1], sharers, cores.shape[1], kv)
        return jnp.sum(group, axis=1).astype(BF16).reshape(kv, kv)

    up = lax.rem(sec + 1, sections)
    down = lax.rem(sec + sections - 1, sections)

    @pl.when(sec == 0)
    def _():
        hop[2] = jnp.zeros((tokens, kv), BF16)

    @pl.when(sec > 0)
    def _():
        copy(mine, hop.at[2], h_send.at[0], h_recv.at[0], (down, me)).wait_recv()

    total = hop[2].astype(F32)
    mean = square + 2 * jnp.sum(total * sums[...], axis=1, keepdims=True)
    mean = (mean + repeat * jnp.sum(total * total, axis=1, keepdims=True)) / width
    scale = lax.rsqrt(jnp.maximum(mean, 0) + epsilon)
    full[...] = (full[...] + dot(hop[2], core(), ((1,), (0,)))) * scale
    mine[...] = (total + full[...]).astype(BF16)

    @pl.when(sec < sections - 1)
    def _():
        copy(mine, hop.at[2], h_send.at[0], h_recv.at[0], (up, me)).start()

    part = shift_ref.shape[2]

    def share_of(dest):
        return pl.ds(pl.multiple_of((dest // sharers) * part, part), part)

    def shift_out(k):
        dest = at(k)
        return copy(hop.at[2, :, share_of(dest)], shift_ref.at[me], v_send.at[k], v_recv.at[me], (sec, dest))

    @pl.loop(1, n)
    def _(k):
        shift_out(k).start()

    local = pltpu.make_async_copy(hop.at[2, :, share_of(me)], shift_ref.at[me], own_sem)
    local.start()

    @pl.when(sec == sections - 1)
    def _():
        hop[1] = hop[0]

    @pl.when(sec < sections - 1)
    def _():
        copy(hop.at[3], hop.at[1], h_send.at[1], h_recv.at[1], (up, me)).wait_recv()

    vgrad = hop[1].astype(F32)

    @pl.when(sec > 0)
    def _():
        along = jnp.sum(vgrad * full[...], axis=1, keepdims=True) / width
        below = vgrad + scale * dot(hop[1], core(), ((1,), (1,)))
        below = below - scale * scale * along * (sums[...] + repeat * hop[2].astype(F32))
        hop[3] = below.astype(BF16)
        copy(hop.at[3], hop.at[1], h_send.at[1], h_recv.at[1], (down, me)).start()

    right_ref[me] = (vgrad * scale).astype(BF16)
    gather_start(right_ref, g_send, f_send, g_recv)

    @pl.loop(1, half_n)
    def _(k):
        gather_forward(right_ref, g_send, f_send, g_recv, k)

    gather_end(right_ref, g_send, f_send, g_recv)
    local.wait()

    @pl.when(sec < sections - 1)
    def _():
        copy(mine, hop.at[2], h_send.at[0], h_recv.at[0], (up, me)).wait_send()

    @pl.when(sec > 0)
    def _():
        copy(hop.at[3], hop.at[1], h_send.at[1], h_recv.at[1], (down, me)).wait_send()

    @pl.loop(1, n)
    def _(k):
        src = at(-k)
        copy(hop.at[2, :, share_of(me)], shift_ref.at[src], v_send.at[k], v_recv.at[src], (sec, src)).wait_recv()
        shift_out(k).wait_send()
        spread_out(k).wait_send()
        share(src, sec, b_send, b_recv, twin).wait_send()
        share(src, sec, e_send, e_recv, across).wait_send()
        share(src, across, p_send, p_recv, twin).wait_send()

    @pl.loop(0, half_n)
    def _(k):
        mate_out(at(2 * k + 1)).wait_send()

    @pl.loop(1, half_n)
    def _(k):
        lane_out(k).wait_send()


def per_device(value_weight, norm_gain, mask_logits, gumbel_noise, stream_in, stream_grad):
    sections = lax.axis_size("section")
    index, n = lax.axis_index("dp"), lax.axis_size("dp")
    micro, rows, width = stream_in.shape
    weight, logits, noise = value_weight[0], mask_logits[0], gumbel_noise[0]
    block, kv = weight.shape
    head = kv // VHEADS
    repeat = width // kv
    local = min(block // head, repeat)
    heads = block // (local * head)
    sharers = n * heads // VHEADS
    share = heads * head
    tokens = micro * rows
    count = n * tokens
    gain = lax.dynamic_slice_in_dim(norm_gain[0], index * block, block, 0).astype(F32)
    steps = block // head
    pattern = pl.BlockSpec((6, head // 4, kv), lambda i: (0, i, 0))
    strip = pl.BlockSpec((head, kv), lambda i: (i, 0))

    masked, core = pl.pallas_call(
        functools.partial(mask_kernel, local, head),
        grid=(steps,),
        out_shape=[jax.ShapeDtypeStruct((block, kv), BF16), jax.ShapeDtypeStruct((share, kv), BF16)],
        in_specs=[pattern, pattern, strip, pl.BlockSpec((head, 1), lambda i: (i, 0))],
        out_specs=[strip, pl.BlockSpec((head, kv), lambda i: (i // local, 0))],
        scratch_shapes=[pltpu.VMEM((head, kv), F32)],
        compiler_params=pltpu.CompilerParams(vmem_limit_bytes=LIMIT),
        name="masks",
    )(logits, noise, weight, gain[:, None])

    dma = pltpu.SemaphoreType.DMA
    vmem = pl.BlockSpec(memory_space=pltpu.VMEM)
    spread, shift, right = pl.pallas_call(
        functools.partial(relay_kernel, n, sections, sharers),
        out_shape=[
            jax.ShapeDtypeStruct((n, tokens, block), BF16),
            jax.ShapeDtypeStruct((n, tokens, share), BF16),
            jax.ShapeDtypeStruct((n, tokens, kv), BF16),
        ],
        in_specs=[vmem] * 5,
        out_specs=[vmem] * 3,
        scratch_shapes=[
            pltpu.VMEM((n, share, kv), BF16),
            pltpu.VMEM((n, tokens, kv), BF16),
            pltpu.VMEM((n // 2, tokens, kv), BF16),
            pltpu.VMEM((n // 2, tokens, kv), BF16),
            pltpu.VMEM((tokens, kv), F32),
            pltpu.VMEM((tokens, kv), F32),
            pltpu.VMEM((4, tokens, kv), BF16),
            pltpu.VMEM((tokens, kv), BF16),
            dma((n,)), dma((n,)), dma((n,)), dma((n,)), dma((n,)), dma((n,)), dma((n,)),
            dma((n,)), dma((n,)), dma((n,)), dma((n,)),
            dma((n,)), dma((n,)), dma((n,)), dma((n,)), dma((2,)), dma((2,)),
            dma((n,)), dma((n,)), dma((n,)), dma((n,)), dma((n,)), dma,
        ],
        compiler_params=pltpu.CompilerParams(collective_id=0, has_side_effects=True, vmem_limit_bytes=LIMIT),
        name="relay",
    )(stream_in.reshape(tokens, width), stream_grad.reshape(tokens, width), gain[None], masked, core)

    out = pl.pallas_call(
        logit_kernel,
        grid=(steps,),
        out_shape=jax.ShapeDtypeStruct(logits.shape, BF16),
        in_specs=[
            pattern,
            pattern,
            strip,
            pl.BlockSpec((1, head), lambda i: (0, i)),
            pl.BlockSpec((count, head), lambda i: (0, i)),
            pl.BlockSpec((count, head), lambda i: (0, i // local)),
            pl.BlockSpec((count, kv), lambda i: (0, 0)),
        ],
        out_specs=pattern,
        compiler_params=pltpu.CompilerParams(vmem_limit_bytes=LIMIT),
        name="logits",
    )(logits, noise, weight, gain[None], spread.reshape(count, block), shift.reshape(count, share), right.reshape(count, kv))
    return out[None]


def solution(mesh):
    return jax.shard_map(
        per_device,
        mesh=mesh,
        in_specs=(
            P("section", "dp", None),
            P("section", None),
            P("section", None, "dp", None),
            P("section", None, "dp", None),
            P(None, "dp", None),
            P(None, "dp", None),
        ),
        out_specs=P("section", None, "dp", None),
        check_vma=False,
    )
```

```python
import functools

import jax
import jax.numpy as jnp
from jax import lax
from jax.experimental import pallas as pl
from jax.experimental.pallas import tpu as pltpu
from jax.sharding import PartitionSpec as P

VHEADS = 8


sharpness_divisor = 0.6666667
epsilon = 1e-05
F32 = jnp.float32
BF16 = jnp.bfloat16
MESH = pl.DeviceIdType.MESH
LIMIT = 60 * 1024 * 1024


def dot(a, b, contract):
    return lax.dot_general(a, b, (contract, ((), ())), preferred_element_type=F32)


def planar(size):
    feature = lax.broadcasted_iota(jnp.int32, (size, size), 0)
    position = lax.broadcasted_iota(jnp.int32, (size, size), 1)
    groups = size // 4
    return (feature == 4 * (position % groups) + position // groups).astype(F32).astype(BF16)


def pattern_probs(logits_ref, noise_ref):
    scores = [
        jnp.exp((logits_ref[k].astype(F32) + noise_ref[k].astype(F32)) / sharpness_divisor) for k in range(6)
    ]
    inverse = 1.0 / (scores[0] + scores[1] + scores[2] + scores[3] + scores[4] + scores[5])
    return [score * inverse for score in scores]


def mask_step(step, head, local, logits_ref, noise_ref, weight_ref, gain_ref, masked_ref, core_ref, total):
    groups = head // 4
    rows = pl.ds(pl.multiple_of(step * head, head), head)
    some = pl.ds(pl.multiple_of(step * groups, groups), groups)
    order = planar(head)
    p = pattern_probs(logits_ref.at[:, some], noise_ref.at[:, some])
    planes = [p[0] + p[1] + p[2], p[0] + p[3] + p[4], p[1] + p[3] + p[5], p[2] + p[4] + p[5]]
    apart = dot(order, weight_ref[rows], ((0,), (0,)))
    kept = [(apart[r * groups:(r + 1) * groups] * planes[r]).astype(BF16) for r in range(4)]
    masked = dot(order, jnp.concatenate(kept, axis=0), ((1,), (0,)))
    masked_ref[rows] = masked.astype(BF16)
    term = masked * gain_ref[rows]

    @pl.when(step % local == 0)
    def _():
        total[...] = term

    @pl.when(step % local != 0)
    def _():
        total[...] += term

    core_ref[pl.ds(pl.multiple_of((step // local) * head, head), head)] = total[...].astype(BF16)


def logit_kernel(logits_ref, noise_ref, weight_ref, gain_ref, spread_ref, shift_ref, right_ref, out_ref):
    size = weight_ref.shape[0]
    groups = size // 4
    order = planar(size)
    left = (spread_ref[...].astype(F32) + shift_ref[...].astype(F32)) * gain_ref[...]
    left = dot(left.astype(BF16), order, ((1,), (0,))).astype(BF16)
    wgrad = dot(left, right_ref[...], ((0,), (0,)))
    grad = wgrad * dot(order, weight_ref[...], ((0,), (0,)))
    a, b, c, d = [grad[r * groups:(r + 1) * groups] for r in range(4)]
    p = pattern_probs(logits_ref, noise_ref)
    dprob = [a + b, a + c, a + d, b + c, b + d, c + d]
    mean = sum(p[k] * dprob[k] for k in range(6))
    for k in range(6):
        out_ref[k] = (p[k] * (dprob[k] - mean) / sharpness_divisor).astype(BF16)


def relay_kernel(
    n, sections, sharers, local, x0_ref, top_ref, gain_ref, logits_ref, noise_ref, weight_ref, column_ref,
    spread_ref, shift_ref, right_ref, masked_ref, running, cores, parts, fromy, fromz, sums, full, hop, mine,
    a_send, a_recv, b_send, b_recv, e_send, e_recv, p_send, p_recv, c_send, c_recv, d_send, y_send, y_recv, z_send, z_recv,
    h_send, h_recv, v_send, v_recv, g_send, g_recv, f_send, own_sem,
):
    me, sec = lax.axis_index("dp"), lax.axis_index("section")
    half_n = n // 2
    lane = me % 2
    mate = me + 1 - 2 * lane
    twin = sec + 1 - 2 * (sec % 2)
    tokens, width = x0_ref.shape
    block = spread_ref.shape[2]
    kv = masked_ref.shape[1]
    head = kv // VHEADS
    repeat = width // kv
    quarter = tokens // 4
    across = lax.rem(sec + 2, sections)
    beyond = lax.rem(twin + 2, sections)
    place = me // 2

    def at(k):
        return lax.rem(me + k + n, n)

    barrier = pltpu.get_barrier_semaphore()

    @pl.loop(1, n)
    def _(k):
        pl.semaphore_signal(barrier, inc=1, device_id=(sec, at(k)), device_id_type=MESH)

    for step in range(1, sections):
        pl.semaphore_signal(barrier, inc=1, device_id=(lax.rem(sec + step, sections), me), device_id_type=MESH)
    pl.semaphore_wait(barrier, n + sections - 2)

    def copy(src, dst, send, recv, where):
        return pltpu.make_async_remote_copy(
            src_ref=src, dst_ref=dst, send_sem=send, recv_sem=recv, device_id=where, device_id_type=MESH
        )

    def quarter_of(which):
        return pl.ds(pl.multiple_of(which * quarter, quarter), quarter)

    def spread_out(k):
        dest = at(k)
        cols = pl.ds(pl.multiple_of(dest * block, block), block)
        rows = quarter_of(sec)
        return copy(x0_ref.at[rows, cols], spread_ref.at[me, rows], a_send.at[k], a_recv.at[me], (sec, dest))

    def share(src, which, send, recv, to):
        ref = spread_ref.at[src, quarter_of(which)]
        return copy(ref, ref, send.at[src], recv.at[src], (to, me))

    def spread_in(src):
        ref = spread_ref.at[src, quarter_of(sec)]
        return copy(ref, ref, a_send.at[0], a_recv.at[src], (sec, mate))

    own_cols = pl.ds(pl.multiple_of(me * block, block), block)
    own = pltpu.make_async_copy(x0_ref.at[:, own_cols], spread_ref.at[me], own_sem)
    own.start()

    @pl.loop(1, n)
    def _(k):
        spread_out(k).start()

    def lane_copy(buf, send, recv, src, slot, dest):
        return copy(buf.at[src], buf.at[src], send.at[slot], recv.at[src], (sec, dest))

    def to_right(buf, send, recv, src, slot):
        return lane_copy(buf, send, recv, src, slot, lax.rem(me + 2, n))

    def to_left(buf, send, recv, src, slot):
        return lane_copy(buf, send, recv, src, slot, lax.rem(me + n - 2, n))

    def gather_pass(buf, more, recv, src):
        return lane_copy(buf, more, recv, src, src, mate)

    def gather_start(buf, send, more, recv):
        @pl.when(place < half_n - 1)
        def _():
            to_right(buf, send, recv, me, me).start()

        @pl.when(place > 0)
        def _():
            to_left(buf, send, recv, me, mate).start()

        gather_pass(buf, more, recv, me).start()

    def gather_forward(buf, send, more, recv, k):
        @pl.when(place >= k)
        def _():
            src = me - 2 * k
            gather_pass(buf, more, recv, src).wait_recv()

            @pl.when(place < half_n - 1)
            def _():
                to_right(buf, send, recv, src, src).start()

            gather_pass(buf, more, recv, src).start()

        @pl.when(place + k < half_n)
        def _():
            src = me + 2 * k
            gather_pass(buf, more, recv, src).wait_recv()

            @pl.when(place > 0)
            def _():
                to_left(buf, send, recv, src, src).start()

            gather_pass(buf, more, recv, src).start()

    def gather_end(buf, send, more, recv):
        @pl.loop(0, half_n)
        def _(k):
            src = 2 * k + lane
            gather_pass(buf, more, recv, 2 * k + 1 - lane).wait_recv()
            gather_pass(buf, more, recv, src).wait_send()

            @pl.when((k <= place) & (place < half_n - 1))
            def _():
                to_right(buf, send, recv, src, src).wait_send()

            @pl.when((k > place) & (place > 0))
            def _():
                to_left(buf, send, recv, src, src).wait_send()

        @pl.when(place > 0)
        def _():
            to_left(buf, send, recv, me, mate).wait_send()

    head_steps = block // head

    @pl.loop(0, head_steps)
    def _(step):
        mask_step(step, head, local, logits_ref, noise_ref, weight_ref, column_ref, masked_ref, cores.at[me], running)

    gather_start(cores, c_send, d_send, c_recv)

    def product(src):
        lhs = (spread_ref[src].astype(F32) * gain_ref[...]).astype(BF16)
        parts[src] = dot(lhs, masked_ref[...], ((1,), (0,))).astype(BF16)

    def mate_out(owner):
        return copy(parts.at[owner], fromy.at[owner // 2], y_send.at[owner // 2], y_recv.at[owner // 2], (sec, mate))

    def mate_in(owner):
        return copy(parts.at[owner], fromy.at[owner // 2], y_send.at[owner // 2], y_recv.at[owner // 2], (sec, mate))

    def arrive(k):
        src = at(-k)
        spread_in(src).wait_recv()
        share(src, sec, e_send, e_recv, across).start()
        share(src, sec, b_send, b_recv, twin).start()

    def cross(k):
        src = at(-k)
        share(src, across, e_send, e_recv, across).wait_recv()
        share(src, across, p_send, p_recv, twin).start()

    def whole(k):
        src = at(-k)
        share(src, twin, b_send, b_recv, twin).wait_recv()
        share(src, beyond, p_send, p_recv, twin).wait_recv()
        product(src)

    arrive(1)
    own.wait()
    product(me)
    arrive(2)
    cross(1)

    folded = []
    tops = []
    square = jnp.zeros((tokens, 1), F32)
    for h in range(VHEADS):
        low = jnp.zeros((tokens, head), F32)
        high = jnp.zeros((tokens, head), F32)
        power = jnp.zeros((tokens, head), F32)
        for r in range(repeat):
            cols = slice((h * repeat + r) * head, (h * repeat + r + 1) * head)
            x = x0_ref[:, cols].astype(F32)
            low = low + x
            power = power + x * x
            high = high + top_ref[:, cols].astype(F32)
        folded.append(low)
        tops.append(high)
        square = square + jnp.sum(power, axis=1, keepdims=True)
    sums[...] = jnp.concatenate(folded, axis=1)
    hop[0] = jnp.concatenate(tops, axis=1).astype(BF16)

    @pl.loop(1, half_n)
    def _(j):
        arrive(2 * j + 1)
        cross(2 * j)
        whole(2 * j - 1)
        mate_out(at(1 - 2 * j)).start()

        @pl.when(j < half_n - 1)
        def _():
            arrive(2 * j + 2)

        cross(2 * j + 1)
        whole(2 * j)
        gather_forward(cores, c_send, d_send, c_recv, j)

    whole(n - 1)
    mate_out(at(1 - n)).start()

    def lane_out(k):
        owner = at(2 * k)
        return copy(parts.at[owner], fromz.at[me // 2], z_send.at[k], z_recv.at[me // 2], (sec, owner))

    def lane_in(src):
        return copy(parts.at[src], fromz.at[src // 2], z_send.at[0], z_recv.at[src // 2], (sec, mate))

    @pl.loop(1, half_n)
    def _(j):
        k = half_n - j
        owner = at(2 * k)
        mate_in(owner).wait_recv()
        parts[owner] = (parts[owner].astype(F32) + fromy[owner // 2].astype(F32)).astype(BF16)
        lane_out(k).start()

    mate_in(me).wait_recv()
    full[...] = parts[me].astype(F32) + fromy[me // 2].astype(F32)

    @pl.loop(1, half_n)
    def _(k):
        src = at(-2 * k)
        lane_in(src).wait_recv()
        full[...] += fromz[src // 2].astype(F32)

    gather_end(cores, c_send, d_send, c_recv)

    def core():
        if sharers == 1:
            return cores[...].reshape(kv, kv)
        group = cores[...].astype(F32).reshape(kv // cores.shape[1], sharers, cores.shape[1], kv)
        return jnp.sum(group, axis=1).astype(BF16).reshape(kv, kv)

    up = lax.rem(sec + 1, sections)
    down = lax.rem(sec + sections - 1, sections)

    @pl.when(sec == 0)
    def _():
        hop[2] = jnp.zeros((tokens, kv), BF16)

    @pl.when(sec > 0)
    def _():
        copy(mine, hop.at[2], h_send.at[0], h_recv.at[0], (down, me)).wait_recv()

    total = hop[2].astype(F32)
    mean = square + 2 * jnp.sum(total * sums[...], axis=1, keepdims=True)
    mean = (mean + repeat * jnp.sum(total * total, axis=1, keepdims=True)) / width
    scale = lax.rsqrt(jnp.maximum(mean, 0) + epsilon)
    full[...] = (full[...] + dot(hop[2], core(), ((1,), (0,)))) * scale
    mine[...] = (total + full[...]).astype(BF16)

    @pl.when(sec < sections - 1)
    def _():
        copy(mine, hop.at[2], h_send.at[0], h_recv.at[0], (up, me)).start()

    part = shift_ref.shape[2]

    def share_of(dest):
        return pl.ds(pl.multiple_of((dest // sharers) * part, part), part)

    def shift_out(k):
        dest = at(k)
        return copy(hop.at[2, :, share_of(dest)], shift_ref.at[me], v_send.at[k], v_recv.at[me], (sec, dest))

    @pl.loop(1, n)
    def _(k):
        shift_out(k).start()

    stay = pltpu.make_async_copy(hop.at[2, :, share_of(me)], shift_ref.at[me], own_sem)
    stay.start()

    @pl.when(sec == sections - 1)
    def _():
        hop[1] = hop[0]

    @pl.when(sec < sections - 1)
    def _():
        copy(hop.at[3], hop.at[1], h_send.at[1], h_recv.at[1], (up, me)).wait_recv()

    vgrad = hop[1].astype(F32)

    @pl.when(sec > 0)
    def _():
        along = jnp.sum(vgrad * full[...], axis=1, keepdims=True) / width
        below = vgrad + scale * dot(hop[1], core(), ((1,), (1,)))
        below = below - scale * scale * along * (sums[...] + repeat * hop[2].astype(F32))
        hop[3] = below.astype(BF16)
        copy(hop.at[3], hop.at[1], h_send.at[1], h_recv.at[1], (down, me)).start()

    right_ref[me] = (vgrad * scale).astype(BF16)
    gather_start(right_ref, g_send, f_send, g_recv)

    @pl.loop(1, half_n)
    def _(k):
        gather_forward(right_ref, g_send, f_send, g_recv, k)

    gather_end(right_ref, g_send, f_send, g_recv)
    stay.wait()

    @pl.when(sec < sections - 1)
    def _():
        copy(mine, hop.at[2], h_send.at[0], h_recv.at[0], (up, me)).wait_send()

    @pl.when(sec > 0)
    def _():
        copy(hop.at[3], hop.at[1], h_send.at[1], h_recv.at[1], (down, me)).wait_send()

    @pl.loop(1, n)
    def _(k):
        src = at(-k)
        copy(hop.at[2, :, share_of(me)], shift_ref.at[src], v_send.at[k], v_recv.at[src], (sec, src)).wait_recv()
        shift_out(k).wait_send()
        spread_out(k).wait_send()
        share(src, sec, b_send, b_recv, twin).wait_send()
        share(src, sec, e_send, e_recv, across).wait_send()
        share(src, across, p_send, p_recv, twin).wait_send()

    @pl.loop(0, half_n)
    def _(k):
        mate_out(at(2 * k + 1)).wait_send()

    @pl.loop(1, half_n)
    def _(k):
        lane_out(k).wait_send()


def per_device(value_weight, norm_gain, mask_logits, gumbel_noise, stream_in, stream_grad):
    sections = lax.axis_size("section")
    index, n = lax.axis_index("dp"), lax.axis_size("dp")
    micro, rows, width = stream_in.shape
    weight, logits, noise = value_weight[0], mask_logits[0], gumbel_noise[0]
    block, kv = weight.shape
    head = kv // VHEADS
    repeat = width // kv
    local = min(block // head, repeat)
    heads = block // (local * head)
    sharers = n * heads // VHEADS
    share = heads * head
    tokens = micro * rows
    count = n * tokens
    gain = lax.dynamic_slice_in_dim(norm_gain[0], index * block, block, 0).astype(F32)
    steps = block // head
    pattern = pl.BlockSpec((6, head // 4, kv), lambda i: (0, i, 0))
    strip = pl.BlockSpec((head, kv), lambda i: (i, 0))

    dma = pltpu.SemaphoreType.DMA
    vmem = pl.BlockSpec(memory_space=pltpu.VMEM)
    spread, shift, right = pl.pallas_call(
        functools.partial(relay_kernel, n, sections, sharers, local),
        out_shape=[
            jax.ShapeDtypeStruct((n, tokens, block), BF16),
            jax.ShapeDtypeStruct((n, tokens, share), BF16),
            jax.ShapeDtypeStruct((n, tokens, kv), BF16),
        ],
        in_specs=[vmem] * 7,
        out_specs=[vmem] * 3,
        scratch_shapes=[
            pltpu.VMEM((block, kv), BF16),
            pltpu.VMEM((head, kv), F32),
            pltpu.VMEM((n, share, kv), BF16),
            pltpu.VMEM((n, tokens, kv), BF16),
            pltpu.VMEM((n // 2, tokens, kv), BF16),
            pltpu.VMEM((n // 2, tokens, kv), BF16),
            pltpu.VMEM((tokens, kv), F32),
            pltpu.VMEM((tokens, kv), F32),
            pltpu.VMEM((4, tokens, kv), BF16),
            pltpu.VMEM((tokens, kv), BF16),
            dma((n,)), dma((n,)), dma((n,)), dma((n,)), dma((n,)), dma((n,)), dma((n,)),
            dma((n,)), dma((n,)), dma((n,)), dma((n,)),
            dma((n,)), dma((n,)), dma((n,)), dma((n,)), dma((2,)), dma((2,)),
            dma((n,)), dma((n,)), dma((n,)), dma((n,)), dma((n,)), dma,
        ],
        compiler_params=pltpu.CompilerParams(collective_id=0, has_side_effects=True, vmem_limit_bytes=LIMIT),
        name="relay",
    )(stream_in.reshape(tokens, width), stream_grad.reshape(tokens, width), gain[None], logits, noise, weight, gain[:, None])

    out = pl.pallas_call(
        logit_kernel,
        grid=(steps,),
        out_shape=jax.ShapeDtypeStruct(logits.shape, BF16),
        in_specs=[
            pattern,
            pattern,
            strip,
            pl.BlockSpec((1, head), lambda i: (0, i)),
            pl.BlockSpec((count, head), lambda i: (0, i)),
            pl.BlockSpec((count, head), lambda i: (0, i // local)),
            pl.BlockSpec((count, kv), lambda i: (0, 0)),
        ],
        out_specs=pattern,
        compiler_params=pltpu.CompilerParams(vmem_limit_bytes=LIMIT),
        name="logits",
    )(logits, noise, weight, gain[None], spread.reshape(count, block), shift.reshape(count, share), right.reshape(count, kv))
    return out[None]


def solution(mesh):
    return jax.shard_map(
        per_device,
        mesh=mesh,
        in_specs=(
            P("section", "dp", None),
            P("section", None),
            P("section", None, "dp", None),
            P("section", None, "dp", None),
            P(None, "dp", None),
            P(None, "dp", None),
        ),
        out_specs=P("section", None, "dp", None),
        check_vma=False,
    )
```

```python
import functools

import jax
import jax.numpy as jnp
from jax import lax
from jax.experimental import pallas as pl
from jax.experimental.pallas import tpu as pltpu
from jax.sharding import PartitionSpec as P

VHEADS = 8


sharpness_divisor = 0.6666667
epsilon = 1e-05
F32 = jnp.float32
BF16 = jnp.bfloat16
MESH = pl.DeviceIdType.MESH
LIMIT = 60 * 1024 * 1024


def dot(a, b, contract):
    return lax.dot_general(a, b, (contract, ((), ())), preferred_element_type=F32)


def planar(size):
    feature = lax.broadcasted_iota(jnp.int32, (size, size), 0)
    position = lax.broadcasted_iota(jnp.int32, (size, size), 1)
    groups = size // 4
    return (feature == 4 * (position % groups) + position // groups).astype(F32).astype(BF16)


def pattern_probs(logits_ref, noise_ref):
    scores = [
        jnp.exp((logits_ref[k].astype(F32) + noise_ref[k].astype(F32)) / sharpness_divisor) for k in range(6)
    ]
    inverse = 1.0 / (scores[0] + scores[1] + scores[2] + scores[3] + scores[4] + scores[5])
    return [score * inverse for score in scores]


def mask_step(step, head, local, logits_ref, noise_ref, weight_ref, gain_ref, masked_ref, core_ref, total):
    groups = head // 4
    rows = pl.ds(pl.multiple_of(step * head, head), head)
    some = pl.ds(pl.multiple_of(step * groups, groups), groups)
    order = planar(head)
    p = pattern_probs(logits_ref.at[:, some], noise_ref.at[:, some])
    planes = [p[0] + p[1] + p[2], p[0] + p[3] + p[4], p[1] + p[3] + p[5], p[2] + p[4] + p[5]]
    apart = dot(order, weight_ref[rows], ((0,), (0,)))
    kept = [(apart[r * groups:(r + 1) * groups] * planes[r]).astype(BF16) for r in range(4)]
    masked = dot(order, jnp.concatenate(kept, axis=0), ((1,), (0,)))
    masked_ref[rows] = masked.astype(BF16)
    term = masked * gain_ref[rows]

    @pl.when(step % local == 0)
    def _():
        total[...] = term

    @pl.when(step % local != 0)
    def _():
        total[...] += term

    core_ref[pl.ds(pl.multiple_of((step // local) * head, head), head)] = total[...].astype(BF16)


def logit_step(step, head, local, logits_ref, noise_ref, weight_ref, gain_ref, spread_ref, shift_ref, right_ref, out_ref):
    groups = head // 4
    n, tokens, kv = right_ref.shape
    rows = pl.ds(pl.multiple_of(step * head, head), head)
    some = pl.ds(pl.multiple_of(step * groups, groups), groups)
    mine = pl.ds(pl.multiple_of((step // local) * head, head), head)
    order = planar(head)
    left = spread_ref[:, :, rows].astype(F32) + shift_ref[:, :, mine].astype(F32)
    left = left.reshape(n * tokens, head) * gain_ref[:, rows]
    left = dot(left.astype(BF16), order, ((1,), (0,))).astype(BF16)
    wgrad = dot(left, right_ref[...].reshape(n * tokens, kv), ((0,), (0,)))
    grad = wgrad * dot(order, weight_ref[rows], ((0,), (0,)))
    a, b, c, d = [grad[r * groups:(r + 1) * groups] for r in range(4)]
    p = pattern_probs(logits_ref.at[:, some], noise_ref.at[:, some])
    dprob = [a + b, a + c, a + d, b + c, b + d, c + d]
    mean = sum(p[k] * dprob[k] for k in range(6))
    for k in range(6):
        out_ref[k, some] = (p[k] * (dprob[k] - mean) / sharpness_divisor).astype(BF16)


def relay_kernel(
    n, sections, sharers, local, x0_ref, top_ref, gain_ref, logits_ref, noise_ref, weight_ref, column_ref,
    out_ref, spread_ref, shift_ref, right_ref, masked_ref, running, cores, parts, fromy, fromz, sums, full, hop, mine,
    a_send, a_recv, b_send, b_recv, e_send, e_recv, p_send, p_recv, c_send, c_recv, d_send, y_send, y_recv, z_send, z_recv,
    h_send, h_recv, v_send, v_recv, g_send, g_recv, f_send, own_sem,
):
    me, sec = lax.axis_index("dp"), lax.axis_index("section")
    half_n = n // 2
    lane = me % 2
    mate = me + 1 - 2 * lane
    twin = sec + 1 - 2 * (sec % 2)
    tokens, width = x0_ref.shape
    block = spread_ref.shape[2]
    kv = masked_ref.shape[1]
    head = kv // VHEADS
    repeat = width // kv
    quarter = tokens // 4
    across = lax.rem(sec + 2, sections)
    beyond = lax.rem(twin + 2, sections)
    place = me // 2

    def at(k):
        return lax.rem(me + k + n, n)

    barrier = pltpu.get_barrier_semaphore()

    @pl.loop(1, n)
    def _(k):
        pl.semaphore_signal(barrier, inc=1, device_id=(sec, at(k)), device_id_type=MESH)

    for step in range(1, sections):
        pl.semaphore_signal(barrier, inc=1, device_id=(lax.rem(sec + step, sections), me), device_id_type=MESH)
    pl.semaphore_wait(barrier, n + sections - 2)

    def copy(src, dst, send, recv, where):
        return pltpu.make_async_remote_copy(
            src_ref=src, dst_ref=dst, send_sem=send, recv_sem=recv, device_id=where, device_id_type=MESH
        )

    def quarter_of(which):
        return pl.ds(pl.multiple_of(which * quarter, quarter), quarter)

    def spread_out(k):
        dest = at(k)
        cols = pl.ds(pl.multiple_of(dest * block, block), block)
        rows = quarter_of(sec)
        return copy(x0_ref.at[rows, cols], spread_ref.at[me, rows], a_send.at[k], a_recv.at[me], (sec, dest))

    def share(src, which, send, recv, to):
        ref = spread_ref.at[src, quarter_of(which)]
        return copy(ref, ref, send.at[src], recv.at[src], (to, me))

    def spread_in(src):
        ref = spread_ref.at[src, quarter_of(sec)]
        return copy(ref, ref, a_send.at[0], a_recv.at[src], (sec, mate))

    own_cols = pl.ds(pl.multiple_of(me * block, block), block)
    own = pltpu.make_async_copy(x0_ref.at[:, own_cols], spread_ref.at[me], own_sem)
    own.start()

    @pl.loop(1, n)
    def _(k):
        spread_out(k).start()

    def lane_copy(buf, send, recv, src, slot, dest):
        return copy(buf.at[src], buf.at[src], send.at[slot], recv.at[src], (sec, dest))

    def to_right(buf, send, recv, src, slot):
        return lane_copy(buf, send, recv, src, slot, lax.rem(me + 2, n))

    def to_left(buf, send, recv, src, slot):
        return lane_copy(buf, send, recv, src, slot, lax.rem(me + n - 2, n))

    def gather_pass(buf, more, recv, src):
        return lane_copy(buf, more, recv, src, src, mate)

    def gather_start(buf, send, more, recv):
        @pl.when(place < half_n - 1)
        def _():
            to_right(buf, send, recv, me, me).start()

        @pl.when(place > 0)
        def _():
            to_left(buf, send, recv, me, mate).start()

        gather_pass(buf, more, recv, me).start()

    def gather_forward(buf, send, more, recv, k):
        @pl.when(place >= k)
        def _():
            src = me - 2 * k
            gather_pass(buf, more, recv, src).wait_recv()

            @pl.when(place < half_n - 1)
            def _():
                to_right(buf, send, recv, src, src).start()

            gather_pass(buf, more, recv, src).start()

        @pl.when(place + k < half_n)
        def _():
            src = me + 2 * k
            gather_pass(buf, more, recv, src).wait_recv()

            @pl.when(place > 0)
            def _():
                to_left(buf, send, recv, src, src).start()

            gather_pass(buf, more, recv, src).start()

    def gather_end(buf, send, more, recv):
        @pl.loop(0, half_n)
        def _(k):
            src = 2 * k + lane
            gather_pass(buf, more, recv, 2 * k + 1 - lane).wait_recv()
            gather_pass(buf, more, recv, src).wait_send()

            @pl.when((k <= place) & (place < half_n - 1))
            def _():
                to_right(buf, send, recv, src, src).wait_send()

            @pl.when((k > place) & (place > 0))
            def _():
                to_left(buf, send, recv, src, src).wait_send()

        @pl.when(place > 0)
        def _():
            to_left(buf, send, recv, me, mate).wait_send()

    head_steps = block // head

    @pl.loop(0, head_steps)
    def _(step):
        mask_step(step, head, local, logits_ref, noise_ref, weight_ref, column_ref, masked_ref, cores.at[me], running)

    gather_start(cores, c_send, d_send, c_recv)

    def product(src):
        lhs = (spread_ref[src].astype(F32) * gain_ref[...]).astype(BF16)
        parts[src] = dot(lhs, masked_ref[...], ((1,), (0,))).astype(BF16)

    def mate_out(owner):
        return copy(parts.at[owner], fromy.at[owner // 2], y_send.at[owner // 2], y_recv.at[owner // 2], (sec, mate))

    def mate_in(owner):
        return copy(parts.at[owner], fromy.at[owner // 2], y_send.at[owner // 2], y_recv.at[owner // 2], (sec, mate))

    def arrive(k):
        src = at(-k)
        spread_in(src).wait_recv()
        share(src, sec, e_send, e_recv, across).start()
        share(src, sec, b_send, b_recv, twin).start()

    def cross(k):
        src = at(-k)
        share(src, across, e_send, e_recv, across).wait_recv()
        share(src, across, p_send, p_recv, twin).start()

    def whole(k):
        src = at(-k)
        share(src, twin, b_send, b_recv, twin).wait_recv()
        share(src, beyond, p_send, p_recv, twin).wait_recv()
        product(src)

    arrive(1)
    own.wait()
    product(me)
    arrive(2)
    cross(1)

    folded = []
    tops = []
    square = jnp.zeros((tokens, 1), F32)
    for h in range(VHEADS):
        low = jnp.zeros((tokens, head), F32)
        high = jnp.zeros((tokens, head), F32)
        power = jnp.zeros((tokens, head), F32)
        for r in range(repeat):
            cols = slice((h * repeat + r) * head, (h * repeat + r + 1) * head)
            x = x0_ref[:, cols].astype(F32)
            low = low + x
            power = power + x * x
            high = high + top_ref[:, cols].astype(F32)
        folded.append(low)
        tops.append(high)
        square = square + jnp.sum(power, axis=1, keepdims=True)
    sums[...] = jnp.concatenate(folded, axis=1)
    hop[0] = jnp.concatenate(tops, axis=1).astype(BF16)

    @pl.loop(1, half_n)
    def _(j):
        arrive(2 * j + 1)
        cross(2 * j)
        whole(2 * j - 1)
        mate_out(at(1 - 2 * j)).start()

        @pl.when(j < half_n - 1)
        def _():
            arrive(2 * j + 2)

        cross(2 * j + 1)
        whole(2 * j)
        gather_forward(cores, c_send, d_send, c_recv, j)

    whole(n - 1)
    mate_out(at(1 - n)).start()

    def lane_out(k):
        owner = at(2 * k)
        return copy(parts.at[owner], fromz.at[me // 2], z_send.at[k], z_recv.at[me // 2], (sec, owner))

    def lane_in(src):
        return copy(parts.at[src], fromz.at[src // 2], z_send.at[0], z_recv.at[src // 2], (sec, mate))

    @pl.loop(1, half_n)
    def _(j):
        k = half_n - j
        owner = at(2 * k)
        mate_in(owner).wait_recv()
        parts[owner] = (parts[owner].astype(F32) + fromy[owner // 2].astype(F32)).astype(BF16)
        lane_out(k).start()

    mate_in(me).wait_recv()
    full[...] = parts[me].astype(F32) + fromy[me // 2].astype(F32)

    @pl.loop(1, half_n)
    def _(k):
        src = at(-2 * k)
        lane_in(src).wait_recv()
        full[...] += fromz[src // 2].astype(F32)

    gather_end(cores, c_send, d_send, c_recv)

    def core():
        if sharers == 1:
            return cores[...].reshape(kv, kv)
        group = cores[...].astype(F32).reshape(kv // cores.shape[1], sharers, cores.shape[1], kv)
        return jnp.sum(group, axis=1).astype(BF16).reshape(kv, kv)

    up = lax.rem(sec + 1, sections)
    down = lax.rem(sec + sections - 1, sections)

    @pl.when(sec == 0)
    def _():
        hop[2] = jnp.zeros((tokens, kv), BF16)

    @pl.when(sec > 0)
    def _():
        copy(mine, hop.at[2], h_send.at[0], h_recv.at[0], (down, me)).wait_recv()

    total = hop[2].astype(F32)
    mean = square + 2 * jnp.sum(total * sums[...], axis=1, keepdims=True)
    mean = (mean + repeat * jnp.sum(total * total, axis=1, keepdims=True)) / width
    scale = lax.rsqrt(jnp.maximum(mean, 0) + epsilon)
    full[...] = (full[...] + dot(hop[2], core(), ((1,), (0,)))) * scale
    mine[...] = (total + full[...]).astype(BF16)

    @pl.when(sec < sections - 1)
    def _():
        copy(mine, hop.at[2], h_send.at[0], h_recv.at[0], (up, me)).start()

    part = shift_ref.shape[2]

    def share_of(dest):
        return pl.ds(pl.multiple_of((dest // sharers) * part, part), part)

    def shift_out(k):
        dest = at(k)
        return copy(hop.at[2, :, share_of(dest)], shift_ref.at[me], v_send.at[k], v_recv.at[me], (sec, dest))

    @pl.loop(1, n)
    def _(k):
        shift_out(k).start()

    stay = pltpu.make_async_copy(hop.at[2, :, share_of(me)], shift_ref.at[me], own_sem)
    stay.start()

    @pl.when(sec == sections - 1)
    def _():
        hop[1] = hop[0]

    @pl.when(sec < sections - 1)
    def _():
        copy(hop.at[3], hop.at[1], h_send.at[1], h_recv.at[1], (up, me)).wait_recv()

    vgrad = hop[1].astype(F32)

    @pl.when(sec > 0)
    def _():
        along = jnp.sum(vgrad * full[...], axis=1, keepdims=True) / width
        below = vgrad + scale * dot(hop[1], core(), ((1,), (1,)))
        below = below - scale * scale * along * (sums[...] + repeat * hop[2].astype(F32))
        hop[3] = below.astype(BF16)
        copy(hop.at[3], hop.at[1], h_send.at[1], h_recv.at[1], (down, me)).start()

    right_ref[me] = (vgrad * scale).astype(BF16)
    gather_start(right_ref, g_send, f_send, g_recv)

    @pl.loop(1, half_n)
    def _(k):
        gather_forward(right_ref, g_send, f_send, g_recv, k)

    gather_end(right_ref, g_send, f_send, g_recv)
    stay.wait()

    @pl.when(sec < sections - 1)
    def _():
        copy(mine, hop.at[2], h_send.at[0], h_recv.at[0], (up, me)).wait_send()

    @pl.when(sec > 0)
    def _():
        copy(hop.at[3], hop.at[1], h_send.at[1], h_recv.at[1], (down, me)).wait_send()

    @pl.loop(1, n)
    def _(k):
        src = at(-k)
        copy(hop.at[2, :, share_of(me)], shift_ref.at[src], v_send.at[k], v_recv.at[src], (sec, src)).wait_recv()
        shift_out(k).wait_send()
        spread_out(k).wait_send()
        share(src, sec, b_send, b_recv, twin).wait_send()
        share(src, sec, e_send, e_recv, across).wait_send()
        share(src, across, p_send, p_recv, twin).wait_send()

    @pl.loop(0, half_n)
    def _(k):
        mate_out(at(2 * k + 1)).wait_send()

    @pl.loop(1, half_n)
    def _(k):
        lane_out(k).wait_send()

    @pl.loop(0, head_steps)
    def _(step):
        logit_step(
            step, head, local, logits_ref, noise_ref, weight_ref, gain_ref, spread_ref, shift_ref, right_ref, out_ref
        )


def per_device(value_weight, norm_gain, mask_logits, gumbel_noise, stream_in, stream_grad):
    sections = lax.axis_size("section")
    index, n = lax.axis_index("dp"), lax.axis_size("dp")
    micro, rows, width = stream_in.shape
    weight, logits, noise = value_weight[0], mask_logits[0], gumbel_noise[0]
    block, kv = weight.shape
    head = kv // VHEADS
    repeat = width // kv
    local = min(block // head, repeat)
    heads = block // (local * head)
    sharers = n * heads // VHEADS
    share = heads * head
    tokens = micro * rows
    gain = lax.dynamic_slice_in_dim(norm_gain[0], index * block, block, 0).astype(F32)

    dma = pltpu.SemaphoreType.DMA
    vmem = pl.BlockSpec(memory_space=pltpu.VMEM)
    out = pl.pallas_call(
        functools.partial(relay_kernel, n, sections, sharers, local),
        out_shape=jax.ShapeDtypeStruct(logits.shape, BF16),
        in_specs=[vmem] * 7,
        out_specs=vmem,
        scratch_shapes=[
            pltpu.VMEM((n, tokens, block), BF16),
            pltpu.VMEM((n, tokens, share), BF16),
            pltpu.VMEM((n, tokens, kv), BF16),
            pltpu.VMEM((block, kv), BF16),
            pltpu.VMEM((head, kv), F32),
            pltpu.VMEM((n, share, kv), BF16),
            pltpu.VMEM((n, tokens, kv), BF16),
            pltpu.VMEM((n // 2, tokens, kv), BF16),
            pltpu.VMEM((n // 2, tokens, kv), BF16),
            pltpu.VMEM((tokens, kv), F32),
            pltpu.VMEM((tokens, kv), F32),
            pltpu.VMEM((4, tokens, kv), BF16),
            pltpu.VMEM((tokens, kv), BF16),
            dma((n,)), dma((n,)), dma((n,)), dma((n,)), dma((n,)), dma((n,)), dma((n,)),
            dma((n,)), dma((n,)), dma((n,)), dma((n,)),
            dma((n,)), dma((n,)), dma((n,)), dma((n,)), dma((2,)), dma((2,)),
            dma((n,)), dma((n,)), dma((n,)), dma((n,)), dma((n,)), dma,
        ],
        compiler_params=pltpu.CompilerParams(collective_id=0, has_side_effects=True, vmem_limit_bytes=LIMIT),
        name="relay",
    )(stream_in.reshape(tokens, width), stream_grad.reshape(tokens, width), gain[None], logits, noise, weight, gain[:, None])

    return out[None]


def solution(mesh):
    return jax.shard_map(
        per_device,
        mesh=mesh,
        in_specs=(
            P("section", "dp", None),
            P("section", None),
            P("section", None, "dp", None),
            P("section", None, "dp", None),
            P(None, "dp", None),
            P(None, "dp", None),
        ),
        out_specs=P("section", None, "dp", None),
        check_vma=False,
    )
```
